32 devices in a mesh: dp: 8 (over z, x), ctx: 4 (over y, core).
Axes of the slice: x: 2, y: 2, z: 4, core: 2. Of those that a mesh axis runs over, the one named last changes fastest.
Arguments:
- inputs: bfloat16 [16, 1024, 768], P('dp', 'ctx'), may hold values from -6 to 6
- encoded: bfloat16 [16, 512, 768], P('dp', 'ctx'), may hold values from -6 to 6
- cotangent: bfloat16 [16, 1024, 768], P('dp', 'ctx'), may hold values from -6 to 6
- norm_gains: float32 [3, 768], replicated, may hold values from 0.5 to 1.5
- rel_table: float32 [32, 12], replicated, may hold values from -4 to 4
- self_q: bfloat16 [768, 768], P('dp', 'ctx'), may hold values from -0.0390625 to 0.0390625
- self_kv: bfloat16 [2, 768, 768], P(None, 'dp', 'ctx'), may hold values from -0.21875 to 0.21875
- self_o: bfloat16 [768, 768], P('dp', 'ctx'), may hold values from -0.875 to 0.875
- cross_q: bfloat16 [768, 768], P('dp', 'ctx'), may hold values from -0.0390625 to 0.0390625
- cross_kv: bfloat16 [2, 768, 768], P(None, 'dp', 'ctx'), may hold values from -0.21875 to 0.21875
- cross_o: bfloat16 [768, 768], P('dp', 'ctx'), may hold values from -0.875 to 0.875
- ffn_in: bfloat16 [2, 768, 2048], P(None, 'dp', 'ctx'), may hold values from -0.21875 to 0.21875
- ffn_out: bfloat16 [2048, 768], P('dp', 'ctx'), may hold values from -0.125 to 0.125
- dec_segments: int32 [16, 1024], P('dp'), may hold values from 0 to 3, as said below
- enc_segments: int32 [16, 512], P('dp'), may hold values from 0 to 3, as said below
- rel_buckets: int32 [1024], replicated, may hold values from 0 to 31, as said below
Outputs:
- output: bfloat16 [16, 1024, 768], P('dp', 'ctx')
- d_inputs: bfloat16 [16, 1024, 768], P('dp', 'ctx')
- d_encoded: bfloat16 [16, 512, 768], P('dp', 'ctx')
- d_norm_gains: float32 [3, 768], replicated
- d_rel_table: float32 [32, 12], replicated
- d_self_q: float32 [768, 768], P('dp', 'ctx')
- d_self_kv: float32 [2, 768, 768], P(None, 'dp', 'ctx')
- d_self_o: float32 [768, 768], P('dp', 'ctx')
- d_cross_q: float32 [768, 768], P('dp', 'ctx')
- d_cross_kv: float32 [2, 768, 768], P(None, 'dp', 'ctx')
- d_cross_o: float32 [768, 768], P('dp', 'ctx')
- d_ffn_in: float32 [2, 768, 2048], P(None, 'dp', 'ctx')
- d_ffn_out: float32 [2048, 768], P('dp', 'ctx')
The draws below stay inside these ranges and needn't reach their ends.
Inputs may be any that keep to these rules, and one draw needn't show every extreme that they name: `dec_segments`: along each sequence the numbers never fall, start at 0 and take every value up to that sequence's largest; a sequence's decoder and encoder tokens use the same set of numbers. In each aligned group of 2 sequences one sequence is a single document and another has four. `enc_segments`: along each sequence the numbers never fall, start at 0 and take every value up to that sequence's largest, the same set as the sequence's decoder tokens. `rel_buckets`: never falls with the distance; 0 at distance 0.
All inputs are finite; a program needn't handle non-finite values.
Results may differ from the reference program's by a relative error of at most 0.025.
The reference program's roundings to bfloat16 on the way count: a program that leaves them out, or rounds other values in their place, can miss the bound.
Values may be sent and summed in bfloat16 or wider, within the bound.
A program may use at most 320 MiB of HBM per device.

```python
import jax
import jax.numpy as jnp
from jax import lax

D = 768
HEADS = 12
HEAD_DIM = 64
FF = 2048
BUCKETS = 32
SEQ_LEN = 1024
ENC_LEN = 512
SEQ_DEV = 2
SEQS = 16


def segment_plan(key):
    keep_flags = jax.random.randint(jax.random.fold_in(key, 101), (SEQS, 3), 0, 2)
    chosen = jax.random.randint(jax.random.fold_in(key, 102), (SEQS // SEQ_DEV,), 0, SEQ_DEV)
    seq_ids = jnp.arange(SEQS)
    picked = jnp.repeat(chosen, SEQ_DEV)
    single = seq_ids % SEQ_DEV == picked
    fuller = seq_ids % SEQ_DEV == (picked + 1) % SEQ_DEV
    keep_flags = jnp.where(fuller[:, None], 1, keep_flags)
    return jnp.where(single[:, None], 0, keep_flags).astype(jnp.int32)


def segment_ids(key, keep_flags, length):
    sub_keys = jax.random.split(key, SEQS)
    bounds = jax.vmap(lambda sub_key: jax.random.permutation(sub_key, length - 1)[:3] + 1)(sub_keys)
    positions = jnp.arange(length)
    crossed = (bounds[:, None, :] <= positions[None, :, None]).astype(jnp.int32)
    return jnp.sum(keep_flags[:, None, :] * crossed, axis=-1).astype(jnp.int32)


def draw_dec_segments(key, part):
    keep_flags = segment_plan(key)
    key = jax.random.fold_in(key, 1)
    return segment_ids(key, keep_flags, SEQ_LEN)


def draw_enc_segments(key, part):
    keep_flags = segment_plan(key)
    key = jax.random.fold_in(key, 2)
    return segment_ids(key, keep_flags, ENC_LEN)


def draw_rel_buckets(key, part):
    key = jax.random.fold_in(key, 3)
    thresholds = jax.random.permutation(key, SEQ_LEN - 1)[:BUCKETS - 1] + 1
    positions = jnp.arange(SEQ_LEN)
    return jnp.sum((thresholds[None, :] <= positions[:, None]).astype(jnp.int32), axis=1).astype(jnp.int32)


def steps_of(key, extent, cuts, low, largest):
    def one(dim, shards_of):
        draws = jax.random.uniform(jax.random.fold_in(jax.random.fold_in(key, 6), dim), (shards_of,), jnp.float32, low / len(cuts), largest / len(cuts))
        return jnp.repeat(jnp.exp(draws), extent[dim] // shards_of).reshape((-1,) + (1,) * (len(extent) - dim - 1))

    loudness = one(*cuts[0])
    for cut in cuts[1:]:
        loudness = loudness * one(*cut)
    return loudness


def scatter_about(key, dims, scale, most, shards=(), kind=jnp.bfloat16):
    array = scale * jax.random.normal(key, dims, jnp.float32)
    if shards:
        array = array * steps_of(key, dims, shards, -0.22, 0.18)
    return jnp.clip(array, -most, most).astype(kind)


def setup_inputs(seed: int = 0) -> dict:
    key_list = jax.random.split(jax.random.key(seed), 17)
    return {
        "inputs": scatter_about(key_list[0], (SEQS, SEQ_LEN, D), 1.0, 6.0, ((0, 8), (1, 4))),
        "encoded": scatter_about(key_list[1], (SEQS, ENC_LEN, D), 1.0, 6.0, ((0, 8), (1, 4))),
        "cotangent": scatter_about(key_list[2], (SEQS, SEQ_LEN, D), 1.0, 6.0, ((0, 8), (1, 4))),
        "norm_gains": jnp.clip(1.0 + 0.1 * jax.random.normal(key_list[3], (3, D), jnp.float32), 0.5, 1.5),
        "rel_table": scatter_about(key_list[4], (BUCKETS, HEADS), 1.0, 4.0, (), jnp.float32),
        "self_q": scatter_about(key_list[5], (D, D), (D * 32) ** -0.5, 0.0390625, ((0, 8), (1, 4))),
        "self_kv": scatter_about(key_list[6], (2, D, D), D ** -0.5, 0.21875, ((1, 8), (2, 4))),
        "self_o": scatter_about(key_list[7], (D, D), (D // 16) ** -0.5, 0.875, ((0, 8), (1, 4))),
        "cross_q": scatter_about(key_list[8], (D, D), (D * 32) ** -0.5, 0.0390625, ((0, 8), (1, 4))),
        "cross_kv": scatter_about(key_list[9], (2, D, D), D ** -0.5, 0.21875, ((1, 8), (2, 4))),
        "cross_o": scatter_about(key_list[10], (D, D), (D // 16) ** -0.5, 0.875, ((0, 8), (1, 4))),
        "ffn_in": scatter_about(key_list[11], (2, D, FF), D ** -0.5, 0.21875, ((1, 8), (2, 4))),
        "ffn_out": scatter_about(key_list[12], (FF, D), FF ** -0.5, 0.125, ((0, 8), (1, 4))),
        "dec_segments": draw_dec_segments(jax.random.fold_in(key_list[16], 71), 0),
        "enc_segments": draw_enc_segments(jax.random.fold_in(key_list[16], 71), 0),
        "rel_buckets": draw_rel_buckets(jax.random.fold_in(key_list[16], 71), 0),
    }


epsilon = 1e-06
masked_score = -1000000000.0
highest = lax.Precision.HIGHEST

@jax.custom_vjp
def low(v):
    return lax.optimization_barrier(v.astype(jnp.bfloat16)).astype(jnp.float32)

@jax.custom_vjp
def low_back(v):
    return v

def low_keep(v):
    return (low(v), None)

def low_pass(kept, grad):
    return (grad,)

def back_keep(v):
    return (v, None)

def back_low(kept, grad):
    return (low(grad),)
low.defvjp(low_keep, low_pass)
low_back.defvjp(back_keep, back_low)

def rounded_both(value):
    return low_back(low(value))

def rms_norm(value, gain):
    return value * lax.rsqrt(lax.optimization_barrier(jnp.mean(value * value, axis=-1, keepdims=True)) + epsilon) * gain

def project(left, right):
    return jnp.dot(left, right, precision=highest)

def attend(queries, key_rows, value_rows, score_bias, visible):
    length = queries.shape[0]
    key_count = key_rows.shape[0]
    split_q = queries.reshape(length, HEADS, HEAD_DIM)
    split_k = key_rows.reshape(key_count, HEADS, HEAD_DIM)
    split_v = value_rows.reshape(key_count, HEADS, HEAD_DIM)
    scores = jnp.einsum('qhd,khd->hqk', split_q, split_k, precision=highest) + score_bias
    scores = low_back(scores)
    scores = jnp.where(visible[None], scores, masked_score)
    exponent = jnp.exp(scores - lax.optimization_barrier(jnp.max(scores, axis=-1, keepdims=True)))
    attn_probs = low(exponent / lax.optimization_barrier(jnp.sum(exponent, axis=-1, keepdims=True)))
    mixed = jnp.einsum('hqk,khd->qhd', attn_probs, split_v, precision=highest)
    return rounded_both(mixed.reshape(length, HEADS * HEAD_DIM))

def layer(resid_in, enc_in, params, dec_seg, enc_seg, rel_buckets):
    gains, table, query_self, keyval_self, output_self, query_cross, keyval_cross, output_cross, ffn_inner, ffn_outer = params
    places = jnp.arange(SEQ_LEN, dtype=jnp.int32)
    distance = jnp.maximum(places[:, None] - places[None, :], 0).astype(jnp.int32)
    score_bias = jnp.transpose(table[rel_buckets[distance]], (2, 0, 1))
    self_visible = (dec_seg[:, None] == dec_seg[None, :]) & (places[None, :] <= places[:, None])
    cross_visible = dec_seg[:, None] == enc_seg[None, :]
    normed_one = low(rms_norm(resid_in, gains[0]))
    attn_one = attend(rounded_both(project(normed_one, query_self)), rounded_both(project(normed_one, keyval_self[0])), rounded_both(project(normed_one, keyval_self[1])), score_bias, self_visible)
    resid_one = resid_in + low_back(project(attn_one, output_self))
    normed_two = low(rms_norm(resid_one, gains[1]))
    attn_two = attend(rounded_both(project(normed_two, query_cross)), rounded_both(project(enc_in, keyval_cross[0])), rounded_both(project(enc_in, keyval_cross[1])), 0.0, cross_visible)
    resid_two = resid_one + low_back(project(attn_two, output_cross))
    normed_three = low(rms_norm(resid_two, gains[2]))
    gate_value = low_back(project(normed_three, ffn_inner[0]))
    up_value = low_back(project(normed_three, ffn_inner[1]))
    middle = low(jax.nn.gelu(gate_value, approximate=True) * up_value)
    return resid_two + low_back(project(middle, ffn_outer))

def reference(inputs, encoded, cotangent, norm_gains, rel_table, self_q, self_kv, self_o, cross_q, cross_kv, cross_o, ffn_in, ffn_out, dec_segments, enc_segments, rel_buckets):
    params = tuple((weight_arg.astype(jnp.float32) for weight_arg in (norm_gains, rel_table, self_q, self_kv, self_o, cross_q, cross_kv, cross_o, ffn_in, ffn_out)))

    def one_sequence(totals, slices):
        resid_in, enc_in, cot_in, dec_seg, enc_seg = slices

        def forward(resid, enc_states, weights):
            return layer(resid, enc_states, weights, dec_seg, enc_seg, rel_buckets)
        result, pullback = jax.vjp(forward, resid_in.astype(jnp.float32), enc_in.astype(jnp.float32), params)
        d_resid, d_enc, d_params = pullback(cot_in.astype(jnp.float32))
        totals = jax.tree.map(jnp.add, totals, d_params)
        return (totals, (result.astype(jnp.bfloat16), d_resid.astype(jnp.bfloat16), d_enc.astype(jnp.bfloat16)))
    zero_grads = jax.tree.map(jnp.zeros_like, params)
    totals, (output, d_inputs, d_encoded) = lax.scan(one_sequence, zero_grads, (inputs, encoded, cotangent, dec_segments, enc_segments))
    return (output, d_inputs, d_encoded) + tuple(totals)
```

```python
import jax
import jax.numpy as jnp
from jax import lax
from jax.experimental import pallas as pl
from jax.experimental.pallas import tpu as pltpu
from jax.sharding import PartitionSpec as P

HEADS = 12


epsilon = 1e-06
masked_score = -1000000000.0
highest = lax.Precision.HIGHEST


def rms_norm(value, gain):
    return value * lax.rsqrt(jnp.mean(value * value, axis=-1, keepdims=True) + epsilon) * gain


def gated_unit(gate_value, up_value):
    return jax.nn.gelu(gate_value, approximate=True) * up_value


def split_heads(value):
    return value.reshape(value.shape[:-1] + (HEADS, value.shape[-1] // HEADS))


def merge_heads(value):
    return value.reshape(value.shape[:-2] + (value.shape[-2] * value.shape[-1],))


def project(value, weight):
    return jnp.einsum("spd,ed->spe", value, weight, preferred_element_type=jnp.float32).astype(
        jnp.bfloat16
    )


def pull_back(grad, weight):
    return jnp.einsum("spe,ed->spd", grad, weight, preferred_element_type=jnp.float32)


def weight_grad(value, grad):
    return jnp.einsum("spd,spe->ed", value, grad, preferred_element_type=jnp.float32)


def skew_kernel(row_ref, plane_ref):
    rows, columns = plane_ref.shape[1:]
    spread = jnp.broadcast_to(row_ref[0], (rows, row_ref.shape[2]))
    plane_ref[0] = pltpu.roll(spread, 0, 1, stride=1, stride_axis=0)[:, :columns]


def skew_rows(table_rows, rows, columns):
    count, width = table_rows.shape
    return pl.pallas_call(
        skew_kernel,
        grid=(count,),
        in_specs=[pl.BlockSpec((1, 1, width), lambda n: (n, 0, 0))],
        out_specs=pl.BlockSpec((1, rows, columns), lambda n: (n, 0, 0)),
        out_shape=jax.ShapeDtypeStruct((count, rows, columns), jnp.float32),
        compiler_params=pltpu.CompilerParams(vmem_limit_bytes=32 * 1024 * 1024),
    )(table_rows[:, None, :])


def gather_group(shards):
    widths = [shard.shape[1] for shard in shards]
    tall = lax.all_gather(jnp.concatenate(shards, axis=1), "dp", axis=0, tiled=True)
    flat = tall.T
    wholes = []
    lower = 0
    for width in widths:
        wholes.append(lax.all_gather(flat[lower : lower + width], "ctx", axis=0, tiled=True))
        lower += width
    return wholes


def reduce_group(grads):
    pieces = [
        lax.psum_scatter(grad.astype(jnp.bfloat16), "ctx", scatter_dimension=0, tiled=True)
        for grad in grads
    ]
    widths = [piece.shape[0] for piece in pieces]
    joined = jnp.concatenate(pieces, axis=0) if len(pieces) > 1 else pieces[0]
    owned = lax.psum_scatter(joined.T, "dp", scatter_dimension=0, tiled=True).astype(jnp.float32)
    blocks = []
    lower = 0
    for width in widths:
        blocks.append(owned[:, lower : lower + width])
        lower += width
    return blocks


def add_tuples(first, second):
    if first is None:
        return tuple(second)
    return tuple((left_item + right_item for left_item, right_item in zip(first, second)))


def score_block(queries, key_rows, score_bias, visible):
    scores = jnp.einsum("sphd,slhd->shpl", queries, key_rows, preferred_element_type=jnp.float32)
    scores = scores + score_bias
    return jnp.where(visible[:, None], scores, masked_score)


def attend_forward(queries, key_rows, value_rows, score_bias, visible):
    scores = score_block(queries, key_rows, score_bias, visible)
    row_max = jnp.max(scores, axis=-1, keepdims=True)
    exponent = jnp.exp(scores - row_max)
    row_total = jnp.sum(exponent, axis=-1, keepdims=True)
    attn_probs = (exponent / row_total).astype(jnp.bfloat16)
    mixed = jnp.einsum(
        "shpl,slhd->sphd", attn_probs, value_rows, preferred_element_type=jnp.float32
    )
    return (merge_heads(mixed).astype(jnp.bfloat16), row_max + jnp.log(row_total))


def attend_backward(queries, key_rows, value_rows, score_bias, visible, log_total, d_mixed):
    scores = score_block(queries, key_rows, score_bias, visible)
    attn_probs = jnp.exp(scores - log_total)
    d_probs = jnp.einsum("sphd,slhd->shpl", d_mixed, value_rows, preferred_element_type=jnp.float32)
    row_delta = jnp.sum(attn_probs * d_probs, axis=-1, keepdims=True)
    d_scores = (attn_probs * (d_probs - row_delta)).astype(jnp.bfloat16)
    d_queries = jnp.einsum(
        "shpl,slhd->sphd", d_scores, key_rows, preferred_element_type=jnp.float32
    )
    d_values = jnp.einsum(
        "shpl,sphd->slhd",
        attn_probs.astype(jnp.bfloat16),
        d_mixed,
        preferred_element_type=jnp.float32,
    )
    d_keys = jnp.einsum("shpl,sphd->slhd", d_scores, queries, preferred_element_type=jnp.float32)
    return (merge_heads(d_queries), merge_heads(d_keys), merge_heads(d_values), d_scores, row_delta)


def on_device(
    inputs,
    encoded,
    cotangent,
    norm_gains,
    rel_table,
    self_q,
    self_kv,
    self_o,
    cross_q,
    cross_kv,
    cross_o,
    ffn_in,
    ffn_out,
    dec_segments,
    enc_segments,
    rel_buckets,
):
    seq_dev = inputs.shape[0]
    pos_dev = inputs.shape[1]
    seq_len = dec_segments.shape[1]
    bucket_count = rel_table.shape[0]
    micro_count = max(1, seq_dev // 4)
    seq_micro = seq_dev // micro_count
    ctx_start = lax.axis_index("ctx") * pos_dev
    query_place = ctx_start + jnp.arange(pos_dev, dtype=jnp.int32)
    key_place = jnp.arange(seq_len, dtype=jnp.int32)
    causal = key_place[None, :] <= query_place[:, None]
    bucket_ids = jnp.arange(bucket_count, dtype=jnp.int32)
    width = -(-(pos_dev + seq_len) // 128) * 128
    offset = jnp.arange(width, dtype=jnp.int32)
    back = jnp.maximum(
        ctx_start + jnp.where(offset < seq_len, -offset, width - offset), 0
    )
    first_place = jnp.sum(
        (rel_buckets[None, :] < bucket_ids[:, None]).astype(jnp.int32), axis=1
    )
    row_bucket = (
        jnp.sum((back[None, :] >= first_place[:, None]).astype(jnp.int32), axis=0) - 1
    )
    bucket_hot = (row_bucket[:, None] == bucket_ids[None, :]).astype(jnp.float32)
    bias_rows = jnp.dot(bucket_hot, rel_table, precision=highest).T
    planes = skew_rows(
        jnp.concatenate([bias_rows, row_bucket[None].astype(jnp.float32)], axis=0),
        pos_dev,
        seq_len,
    )
    score_bias = planes[:HEADS]
    pair_hot = (planes[HEADS][None] == bucket_ids.astype(jnp.float32)[:, None, None]).astype(
        jnp.float32
    )
    query_self, key_self, value_self = gather_group([self_q, self_kv[0], self_kv[1]])
    key_cross, value_cross, output_self, query_cross, output_cross = gather_group(
        [cross_kv[0], cross_kv[1], self_o, cross_q, cross_o]
    )
    gate_inner, up_inner = gather_group([ffn_in[0], ffn_in[1]])
    (ffn_outer,) = gather_group([ffn_out])
    gain_grads = jnp.zeros_like(norm_gains)
    table_grads = jnp.zeros_like(rel_table)
    whole = None
    output_parts = []
    d_input_parts = []
    d_encoded_parts = []
    for micro_index in range(micro_count):
        lower = micro_index * seq_micro
        upper = lower + seq_micro
        hidden_in = inputs[lower:upper]
        enc_rows = encoded[lower:upper]
        cot_rows = cotangent[lower:upper]
        seg_keys = dec_segments[lower:upper]
        seg_enc = enc_segments[lower:upper]
        seg_query = lax.dynamic_slice_in_dim(seg_keys, ctx_start, pos_dev, 1)
        self_mask = (seg_query[:, :, None] == seg_keys[:, None, :]) & causal[None]
        cross_mask = seg_query[:, :, None] == seg_enc[:, None, :]
        resid_in = hidden_in.astype(jnp.float32)
        normed_one = rms_norm(resid_in, norm_gains[0]).astype(jnp.bfloat16)
        queries_one = jnp.einsum("spd,ed->spe", normed_one, query_self, preferred_element_type=jnp.float32).astype(
            jnp.bfloat16
        )
        keyval_one = jnp.stack([project(normed_one, key_self), project(normed_one, value_self)])
        keyval_two = jnp.stack([project(enc_rows, key_cross), project(enc_rows, value_cross)])
        keyval_one_all, keyval_two_all = (
            lax.all_gather(keyval_one, "ctx", axis=2, tiled=True),
            lax.all_gather(keyval_two, "ctx", axis=2, tiled=True),
        )
        keys_one = split_heads(keyval_one_all[0])
        values_one = split_heads(keyval_one_all[1])
        keys_two = split_heads(keyval_two_all[0])
        values_two = split_heads(keyval_two_all[1])
        attn_one, log_one = attend_forward(
            split_heads(queries_one), keys_one, values_one, score_bias, self_mask
        )
        resid_one = resid_in + jnp.einsum("spd,ed->spe", attn_one, output_self, preferred_element_type=jnp.float32)
        normed_two = rms_norm(resid_one, norm_gains[1]).astype(jnp.bfloat16)
        queries_two = jnp.einsum("spd,ed->spe", normed_two, query_cross, preferred_element_type=jnp.float32).astype(
            jnp.bfloat16
        )
        attn_two, log_two = attend_forward(
            split_heads(queries_two), keys_two, values_two, 0.0, cross_mask
        )
        resid_two = resid_one + jnp.einsum("spd,ed->spe", attn_two, output_cross, preferred_element_type=jnp.float32)
        normed_three = rms_norm(resid_two, norm_gains[2]).astype(jnp.bfloat16)
        gate_up = [
            jnp.einsum("spd,fd->spf", normed_three, inner, preferred_element_type=jnp.float32)
            for inner in (gate_inner, up_inner)
        ]
        middle = gated_unit(gate_up[0], gate_up[1]).astype(jnp.bfloat16)
        result = resid_two + jnp.einsum("spf,df->spd", middle, ffn_outer, preferred_element_type=jnp.float32)
        output_parts.append(result.astype(jnp.bfloat16))
        grad_out = cot_rows.astype(jnp.float32)
        g_ffn_outer = jnp.einsum(
            "spf,spd->df", middle, cot_rows, preferred_element_type=jnp.float32
        )
        d_middle = jnp.einsum(
            "spd,df->spf", cot_rows, ffn_outer, preferred_element_type=jnp.float32
        )
        unit_out, unit_pull = jax.vjp(gated_unit, gate_up[0], gate_up[1])
        d_gate, d_up = unit_pull(d_middle)
        d_gate = d_gate.astype(jnp.bfloat16)
        d_up = d_up.astype(jnp.bfloat16)
        g_gate_inner = weight_grad(normed_three, d_gate)
        g_up_inner = weight_grad(normed_three, d_up)
        d_normed_three = pull_back(d_gate, gate_inner) + pull_back(d_up, up_inner)
        norm_out, norm_pull = jax.vjp(rms_norm, resid_two, norm_gains[2])
        d_resid, d_gain_three = norm_pull(d_normed_three)
        d_resid_two = grad_out + d_resid
        d_cross_out = d_resid_two.astype(jnp.bfloat16)
        g_output_cross = weight_grad(attn_two, d_cross_out)
        d_attn_two = pull_back(d_cross_out, output_cross).astype(jnp.bfloat16)
        d_queries_two, d_keys_two, d_values_two, unused_scores, delta_two = attend_backward(
            split_heads(queries_two),
            keys_two,
            values_two,
            0.0,
            cross_mask,
            log_two,
            split_heads(d_attn_two),
        )
        d_queries_two = d_queries_two.astype(jnp.bfloat16)
        g_query_cross = weight_grad(normed_two, d_queries_two)
        d_normed_two = pull_back(d_queries_two, query_cross)
        norm_out, norm_pull = jax.vjp(rms_norm, resid_one, norm_gains[1])
        d_resid, d_gain_two = norm_pull(d_normed_two)
        d_resid_one = d_resid_two + d_resid
        d_self_out = d_resid_one.astype(jnp.bfloat16)
        g_output_self = weight_grad(attn_one, d_self_out)
        d_attn_one = pull_back(d_self_out, output_self).astype(jnp.bfloat16)
        d_queries_one, d_keys_one, d_values_one, d_scores_one, delta_one = attend_backward(
            split_heads(queries_one),
            keys_one,
            values_one,
            score_bias,
            self_mask,
            log_one,
            split_heads(d_attn_one),
        )
        d_queries_one = d_queries_one.astype(jnp.bfloat16)
        score_sums = jnp.sum(d_scores_one, axis=0, dtype=jnp.float32)
        table_grads = table_grads + jnp.einsum(
            "bpl,hpl->bh", pair_hot, score_sums, precision=highest
        )
        d_keyval_one, d_keyval_two = (
            lax.psum_scatter(
                jnp.stack([d_keys_one, d_values_one]).astype(jnp.bfloat16),
                "ctx",
                scatter_dimension=2,
                tiled=True,
            ).astype(jnp.float32),
            lax.psum_scatter(
                jnp.stack([d_keys_two, d_values_two]).astype(jnp.bfloat16),
                "ctx",
                scatter_dimension=2,
                tiled=True,
            ).astype(jnp.float32),
        )
        d_keyval_one = d_keyval_one.astype(jnp.bfloat16)
        d_keyval_two = d_keyval_two.astype(jnp.bfloat16)
        g_query_self = weight_grad(normed_one, d_queries_one)
        g_key_self = weight_grad(normed_one, d_keyval_one[0])
        g_value_self = weight_grad(normed_one, d_keyval_one[1])
        d_normed_one = pull_back(d_queries_one, query_self)
        d_normed_one = (
            d_normed_one
            + pull_back(d_keyval_one[0], key_self)
            + pull_back(d_keyval_one[1], value_self)
        )
        norm_out, norm_pull = jax.vjp(rms_norm, resid_in, norm_gains[0])
        d_resid, d_gain_one = norm_pull(d_normed_one)
        d_input_parts.append((d_resid_one + d_resid).astype(jnp.bfloat16))
        g_key_cross = weight_grad(enc_rows, d_keyval_two[0])
        g_value_cross = weight_grad(enc_rows, d_keyval_two[1])
        d_encoded_rows = pull_back(d_keyval_two[0], key_cross) + pull_back(
            d_keyval_two[1], value_cross
        )
        d_encoded_parts.append(d_encoded_rows.astype(jnp.bfloat16))
        gain_grads = gain_grads + jnp.stack([d_gain_one, d_gain_two, d_gain_three])
        micro_grads = (
            g_ffn_outer,
            g_gate_inner,
            g_up_inner,
            g_output_cross,
            g_query_cross,
            g_output_self,
            g_key_cross,
            g_value_cross,
            g_query_self,
            g_key_self,
            g_value_self,
        )
        whole = add_tuples(whole, micro_grads)
    (o_ffn_outer,) = reduce_group(whole[:1])
    o_ffn_inner = jnp.stack(reduce_group(whole[1:3]))
    o_output_cross, o_query_cross, o_output_self = reduce_group(whole[3:6])
    o_key_cross, o_value_cross, o_query_self, o_key_self, o_value_self = reduce_group(whole[6:])
    owned = (
        o_query_self,
        jnp.stack([o_key_self, o_value_self]),
        o_output_self,
        o_query_cross,
        jnp.stack([o_key_cross, o_value_cross]),
        o_output_cross,
        o_ffn_inner,
        o_ffn_outer,
    )
    gain_total, table_total = lax.psum((gain_grads, table_grads), ("dp", "ctx"))
    return (
        jnp.concatenate(output_parts, axis=0),
        jnp.concatenate(d_input_parts, axis=0),
        jnp.concatenate(d_encoded_parts, axis=0),
        gain_total,
        table_total,
    ) + owned


def solution(mesh):
    placed = (
        P("dp", "ctx", None),
        P("dp", "ctx", None),
        P("dp", "ctx", None),
        P(),
        P(),
        P("dp", "ctx"),
        P(None, "dp", "ctx"),
        P("dp", "ctx"),
        P("dp", "ctx"),
        P(None, "dp", "ctx"),
        P("dp", "ctx"),
        P(None, "dp", "ctx"),
        P("dp", "ctx"),
        P("dp", None),
        P("dp", None),
        P(),
    )
    return jax.shard_map(
        on_device,
        mesh=mesh,
        in_specs=placed,
        out_specs=(
            P("dp", "ctx", None),
            P("dp", "ctx", None),
            P("dp", "ctx", None),
            P(),
            P(),
            P("dp", "ctx"),
            P(None, "dp", "ctx"),
            P("dp", "ctx"),
            P("dp", "ctx"),
            P(None, "dp", "ctx"),
            P("dp", "ctx"),
            P(None, "dp", "ctx"),
            P("dp", "ctx"),
        ),
        check_vma=False,
    )
```
